32 devices in a mesh: dp: 2 (over x), expert: 16 (over z, y, core).
Axes of the slice: x: 2, y: 2, z: 4, core: 2. Of those that a mesh axis runs over, the one named last changes fastest.
Arguments:
- tokens: bfloat16 [4096, 3584], P(('dp', 'expert')), may hold values from -6 to 6
- out_grad: bfloat16 [4096, 3584], P(('dp', 'expert')), may hold values from -1.1953125 to 1.1953125
- gate_weight: bfloat16 [3584, 8192], P('dp', 'expert'), may hold values from -0.09375 to 0.09375
- up_weight: bfloat16 [3584, 8192], P('dp', 'expert'), may hold values from -0.09375 to 0.09375
- route_ids: int32 [4096, 8], P(('dp', 'expert')), may hold values from 0 to 255, all different within a row; in each aligned block of 128 rows (0 to 127, 128 to 255, ...) at most 6 rows name the same one
- route_weights: float32 [4096, 8], P(('dp', 'expert')), may hold values from 0.02 to 0.5
Outputs:
- grad_down: bfloat16 [8192, 3584], P(('expert', 'dp'))
The draws below stay inside these ranges and needn't reach their ends.
Inputs may be any that keep to these rules, and one draw needn't show every extreme that they name: `route_ids`: each row names 8 different experts. At most 6 of the rows of one device name any one expert, a bound that some block reaches.
All inputs are finite; a program needn't handle non-finite values.
Results may differ from the reference program's by a relative error of at most 0.015.
Values may be sent and summed in bfloat16 or wider, within the bound.
No kernel may reach another device: no remote copies, remote signals or barrier semaphores. Data moves between devices by JAX's collectives and lax.ppermute only.
A program may use at most 128 MiB of HBM per device.

```python
import math
from functools import partial
import jax
import jax.numpy as jnp
import numpy as np
from jax import lax

DW = 3584
FF = 2048
N_ROUTED = 256
TOPK = 8
TOK_DEV = 128
CAP = 6
EXPERTS = 4
TOKENS = 4096
N_DP = 2
N_EXPERT = 16


def shard_levels(own_key, extent, split, smallest, largest):
    gain = 1.0
    for axis_at, blocks in split:
        draws = jax.random.uniform(jax.random.fold_in(jax.random.fold_in(own_key, 6), axis_at), (blocks,), jnp.float32, smallest / len(split), largest / len(split))
        gain = gain * jnp.repeat(jnp.exp(draws), extent[axis_at] // blocks).reshape((-1,) + (1,) * (len(extent) - 1 - axis_at))
    return gain


def routed_block(rng, own, number, rows, count, top, limit, slope):
    ranking = jax.random.permutation(rng, count)
    packed, usual = load_shares(count, rows * top, limit, slope, True), load_shares(count, rows * top, limit, slope, False)
    places = jnp.arange(count)

    def named(lengths, offset_by):
        used = int((lengths > 0).sum())
        fixed = max(1, used // 4)
        moved = fixed + (places - fixed + offset_by * (used - fixed)) % max(1, count - fixed)
        return jnp.zeros((count,), jnp.int32).at[ranking[jnp.where(places < fixed, places, moved)]].set(jnp.asarray(lengths, jnp.int32))

    lengths = jnp.where(number % 4 == 0, named(packed, number // 4), named(usual, number - number // 4 - 1))
    mixed = jax.random.permutation(jax.random.fold_in(own, 3), count)
    source_of, receiver = mixed[0:count // 2 * 2:2], mixed[1:count // 2 * 2:2]
    margin = jnp.minimum(lengths[source_of] - 1, limit - lengths[receiver]) // 2
    margin = jnp.where((source_of == ranking[0]) | (receiver == ranking[0]) | (lengths[receiver] == 0), 0, jnp.maximum(margin, 0))
    moved = jax.random.randint(jax.random.fold_in(own, 4), (count // 2,), 0, 1 << 20) % (margin + 1)
    lengths = lengths.at[source_of].add(-moved).at[receiver].add(moved)
    labels = jnp.searchsorted(jnp.cumsum(lengths), jnp.arange(rows * top), side="right").astype(jnp.int32)
    listing = labels.reshape(top, rows).T
    listing = listing[jax.random.permutation(jax.random.fold_in(own, 1), rows)]
    offset_by = jax.random.randint(jax.random.fold_in(own, 2), (rows, 1), 0, top)
    return jnp.take_along_axis(listing, (jnp.arange(top)[None, :] + offset_by) % top, axis=1)


def load_shares(count, total, bound, lean, full):
    weights = [(1 << 20) // math.isqrt(standing ** lean) + 1 for standing in range(1, count + 1)]
    largest = bound if full else min(bound, max(-(-total // count), total * weights[0] // sum(weights)))
    least = 1 if total - largest >= count - 1 else 0
    holding, rest = [largest] + [least] * (count - 1), total - largest - least * (count - 1)
    while rest > 0:
        movable = [i for i in range(1, count) if holding[i] < largest] or [i for i in range(1, count) if holding[i] < bound]
        whole, remaining = sum([weights[i] for i in movable]), rest
        for i in movable:
            extra = min(bound - holding[i], max(1, remaining * weights[i] // whole), rest)
            holding[i] = holding[i] + extra
            rest = rest - extra
    return np.array(holding)


def gaussian(own_key, extent, width, bound, split=(), held_as=jnp.bfloat16):
    drawn = width * jax.random.normal(own_key, extent, jnp.float32)
    if split:
        drawn = drawn * shard_levels(own_key, extent, split, -0.22, 0.18)
    return jnp.clip(drawn, -bound, bound).astype(held_as)


def setup_inputs(seed: int = 0) -> dict:
    arg_keys = jax.random.split(jax.random.key(seed), 7)
    tokens = gaussian(arg_keys[0], (TOKENS, DW), 1.0, 6.0, ((0, 32),))
    out_grad = gaussian(arg_keys[1], (TOKENS, DW), 0.2, 1.1953125, ((0, 32),))
    gate_weight = gaussian(arg_keys[2], (DW, EXPERTS * FF), DW ** -0.5, 0.09375, ((0, 2), (1, 16)))
    up_weight = gaussian(arg_keys[3], (DW, EXPERTS * FF), DW ** -0.5, 0.09375, ((0, 2), (1, 16)))
    route_ids_keys = jax.random.split(jax.random.fold_in(arg_keys[4], 1), TOKENS // TOK_DEV)
    route_ids_turns = jax.random.permutation(jax.random.fold_in(arg_keys[4], 3), TOKENS // TOK_DEV)
    route_ids = jax.vmap(lambda own, number: routed_block(jax.random.fold_in(arg_keys[4], 2), own, number, TOK_DEV, N_ROUTED, TOPK, CAP, 2))(route_ids_keys, route_ids_turns).reshape((TOKENS, TOPK))
    route_weights = jnp.clip(jnp.exp(math.log(0.5) - 3.218876 * jax.random.uniform(arg_keys[5], (TOKENS, TOPK), jnp.float32) ** shard_levels(arg_keys[5], (TOKENS, TOPK), ((0, 32),), -0.2, 0.2)), 0.02, 0.5)
    return {"tokens": tokens, "out_grad": out_grad, "gate_weight": gate_weight, "up_weight": up_weight, "route_ids": route_ids, "route_weights": route_weights}


def expert_part(expert, group_tokens, group_grads, group_ids, group_weights, gate_weight, up_weight):
    slot_count = N_EXPERT * CAP
    matches = group_ids == expert
    chosen = jnp.any(matches, axis=1)
    scales = jnp.sum(jnp.where(matches, group_weights, 0.0), axis=1)
    picked = jnp.nonzero(chosen, size=slot_count, fill_value=0)[0]
    filled = jnp.arange(slot_count) < jnp.sum(chosen.astype(jnp.int32))
    routed = jnp.where(filled[:, None], group_tokens[picked], jnp.zeros((), jnp.bfloat16))
    scaled = jnp.where(filled[:, None], scales[picked][:, None] * group_grads[picked].astype(jnp.float32), 0.0)
    scaled = scaled.astype(jnp.bfloat16)
    start_col = (expert * FF).astype(jnp.int32)
    gate_cols = lax.dynamic_slice_in_dim(gate_weight, start_col, FF, 1)
    up_cols = lax.dynamic_slice_in_dim(up_weight, start_col, FF, 1)
    gate_pre = jnp.dot(routed, gate_cols, preferred_element_type=jnp.float32)
    up_pre = jnp.dot(routed, up_cols, preferred_element_type=jnp.float32)
    hidden = (jax.nn.silu(gate_pre) * up_pre).astype(jnp.bfloat16)
    return jnp.dot(hidden.T, scaled, preferred_element_type=jnp.float32).astype(jnp.bfloat16)


def reference(tokens, out_grad, gate_weight, up_weight, route_ids, route_weights):
    group_rows = N_EXPERT * TOK_DEV
    token_groups = tokens.reshape(N_DP, group_rows, DW)
    grad_groups = out_grad.reshape(N_DP, group_rows, DW)
    id_groups = route_ids.reshape(N_DP, group_rows, TOPK)
    weight_groups = route_weights.reshape(N_DP, group_rows, TOPK)

    def group_step(running, group_data):
        group_tokens, group_grads, group_ids, group_weights = group_data
        worker = partial(expert_part, group_tokens=group_tokens, group_grads=group_grads, group_ids=group_ids, group_weights=group_weights, gate_weight=gate_weight, up_weight=up_weight)
        partials = lax.map(worker, jnp.arange(EXPERTS, dtype=jnp.int32))
        return running + partials.astype(jnp.float32), None

    start_sum = jnp.zeros((EXPERTS, FF, DW), jnp.float32)
    summed, _ = lax.scan(group_step, start_sum, (token_groups, grad_groups, id_groups, weight_groups))
    return summed.reshape(EXPERTS * FF, DW).astype(jnp.bfloat16)
```

```python
import jax
import jax.numpy as jnp
from jax import lax
from jax.sharding import PartitionSpec as P

N_ROUTED = 256
SPLIT = 4
AXES = ("dp", "expert")


def pack_rows(tokens, out_grad, route_ids, route_weights, experts, row_cap):
    expert_ids = jnp.arange(experts, dtype=jnp.int32)
    matches = route_ids[:, :, None] == expert_ids[None, None, :]
    chosen = jnp.any(matches, axis=1)
    scales = jnp.sum(jnp.where(matches, route_weights[:, :, None], 0.0), axis=1)
    rank = jnp.cumsum(chosen.astype(jnp.int32), axis=0) - 1
    slots = jnp.arange(row_cap, dtype=jnp.int32)
    pick = chosen.T[:, None, :] & (rank.T[:, None, :] == slots[None, :, None])
    flat = pick.reshape(experts * row_cap, tokens.shape[0]).astype(jnp.bfloat16)
    rows = jnp.dot(flat, tokens, preferred_element_type=jnp.float32).astype(jnp.bfloat16)
    grads = jnp.dot(flat, out_grad, preferred_element_type=jnp.float32)
    slot_scales = jnp.sum(jnp.where(pick, scales.T[:, None, :], 0.0), axis=2)
    scaled = (grads * slot_scales.reshape(experts * row_cap, 1)).astype(jnp.bfloat16)
    return rows, scaled


def per_device(tokens, out_grad, gate_weight, up_weight, route_ids, route_weights):
    n_dp, n_expert = lax.axis_size("dp"), lax.axis_size("expert")
    experts = n_expert // SPLIT
    features = tokens.shape[1]
    depth = gate_weight.shape[0]
    units = gate_weight.shape[1]
    own_units = units // n_dp
    cap = max(2, tokens.shape[0] * route_ids.shape[1] * 3 // (2 * N_ROUTED))
    me_d, me_s = lax.axis_index("dp"), lax.axis_index("expert")
    me_e = me_s // SPLIT

    def send(value, by_d, by_e, by_q):
        pairs = []
        for d in range(n_dp):
            for s in range(n_expert):
                e, q = s // SPLIT, s % SPLIT
                to = ((e + by_e) % experts) * SPLIT + (q ^ by_q)
                pairs.append((d * n_expert + s, (d + by_d) % n_dp * n_expert + to))
        return lax.ppermute(value, AXES, pairs)

    rows, scaled = pack_rows(tokens, out_grad, route_ids, route_weights, experts, cap)
    both = jnp.concatenate(
        [rows.reshape(experts, cap, features), scaled.reshape(experts, cap, features)], axis=2
    )

    def block_for(by_e):
        to = (me_e + by_e) % experts
        return lax.dynamic_index_in_dim(both, to, 0, keepdims=False)

    parts = [block_for(0)] + [send(block_for(k), 0, k, 0) for k in range(1, experts)]
    held = jnp.concatenate(parts, axis=0)
    held_x, held_dy = held[:, :features], held[:, features:]

    def x_for(by_d):
        return lax.dynamic_slice_in_dim(held_x, (me_d + by_d) % n_dp * depth, depth, 1)

    x_blocks, dy_blocks = [], []
    for by_d in range(n_dp):
        x_part = x_for(by_d)
        for by_q in range(0, SPLIT, 2):
            x_got = x_part if by_d == by_q == 0 else send(x_part, by_d, 0, by_q)
            x_blocks += [x_got, send(x_got, 0, 0, 1)]
    for by_d in range(n_dp):
        for by_q in range(0, SPLIT, 2):
            dy_got = held_dy if by_d == by_q == 0 else send(held_dy, by_d, 0, by_q)
            dy_blocks += [dy_got, send(dy_got, 0, 0, 1)]
    x_all = jnp.concatenate(x_blocks, axis=0)
    dy_all = jnp.concatenate(dy_blocks, axis=0)

    group_rows = SPLIT * held.shape[0]

    def partial_pre(by_d):
        at = (me_d + by_d) % n_dp * own_units
        gate = lax.dynamic_slice_in_dim(gate_weight, at, own_units, 1)
        up = lax.dynamic_slice_in_dim(up_weight, at, own_units, 1)
        weight = jnp.concatenate([gate, up], axis=1)
        return jnp.dot(x_all, weight, preferred_element_type=jnp.float32)

    arrived = []
    for by_d in range(1, n_dp):
        ready = jnp.roll(partial_pre(by_d), by_d * group_rows, axis=0).astype(jnp.bfloat16)
        arrived.append(send(ready, by_d, 0, 0))
    total = partial_pre(0)
    for other in arrived:
        total = total + other.astype(jnp.float32)
    gate_pre, up_pre = total[:, :own_units], total[:, own_units:]
    hidden = (jax.nn.silu(gate_pre) * up_pre).astype(jnp.bfloat16)
    return lax.dot_general(
        hidden, dy_all, (((0,), (0,)), ((), ())), preferred_element_type=jnp.float32
    ).astype(jnp.bfloat16)


def solution(mesh):
    return jax.shard_map(
        per_device,
        mesh=mesh,
        in_specs=(
            P(("dp", "expert"), None),
            P(("dp", "expert"), None),
            P("dp", "expert"),
            P("dp", "expert"),
            P(("dp", "expert"), None),
            P(("dp", "expert"), None),
        ),
        out_specs=P(("expert", "dp"), None),
        check_vma=False,
    )
```

```python
import functools

import jax
import jax.numpy as jnp
from jax import lax
from jax.experimental import pallas as pl
from jax.experimental.pallas import tpu as pltpu
from jax.sharding import PartitionSpec as P

N_ROUTED = 256
SPLIT = 4
PIECES = 4
AXES = ("dp", "expert")
MIB = 1024 * 1024


def pack_kernel(cap, experts, me_ref, *refs):
    sources, out_refs = refs[:4], refs[4 : 4 + experts]
    held_refs, sems = refs[4 + experts : 8 + experts], refs[8 + experts]
    copies = [
        pltpu.make_async_copy(source, held, sems.at[i])
        for i, (source, held) in enumerate(zip(sources, held_refs))
    ]
    for copy in copies:
        copy.start()
    ids_ref, weights_ref, tokens_ref, grads_ref = held_refs
    rows, width = tokens_ref.shape[0], tokens_ref.shape[1] // PIECES
    copies[0].wait()
    copies[1].wait()
    ids, weights = ids_ref[...], weights_ref[...]
    chosen, scales = [], []
    for k in range(experts):
        match = ids == (me_ref[0] ^ k)
        chosen.append(jnp.max(jnp.where(match, 1.0, 0.0), axis=0, keepdims=True))
        scales.append(jnp.sum(jnp.where(match, weights, 0.0), axis=0, keepdims=True))
    flags = jnp.concatenate(chosen, axis=0)
    before = lax.broadcasted_iota(jnp.int32, (rows, rows), 0)
    after = lax.broadcasted_iota(jnp.int32, (rows, rows), 1)
    upper = jnp.where(before <= after, 1.0, 0.0).astype(jnp.bfloat16)
    rank = jnp.dot(flags.astype(jnp.bfloat16), upper, preferred_element_type=jnp.float32)
    height = PIECES * cap
    row = lax.broadcasted_iota(jnp.int32, (height, rows), 0)
    piece, slot = row // cap, row % cap
    picks, slot_scales = [], []
    for k in range(experts):
        place = jnp.where(chosen[k] > 0.0, rank[k : k + 1], 0.0).astype(jnp.int32)
        pick = place == slot + 1
        picks.append(jnp.where(pick, 1.0, 0.0))
        slot_scales.append(jnp.sum(jnp.where(pick, scales[k], 0.0), axis=1, keepdims=True))
    pick_all = jnp.concatenate(picks, axis=0)
    piece_all = jnp.concatenate([piece] * experts, axis=0)
    select = jnp.concatenate(
        [jnp.where(piece_all == j, pick_all, 0.0) for j in range(PIECES)], axis=1
    ).astype(jnp.bfloat16)

    def pieces(ref):
        return jnp.concatenate([ref[:, j * width : (j + 1) * width] for j in range(PIECES)], axis=0)

    copies[2].wait()
    rows_x = jnp.dot(select, pieces(tokens_ref), preferred_element_type=jnp.float32)
    copies[3].wait()
    rows_dy = jnp.dot(select, pieces(grads_ref), preferred_element_type=jnp.float32)
    for k in range(experts):
        at = slice(k * height, (k + 1) * height)
        both = jnp.concatenate([rows_x[at], rows_dy[at] * slot_scales[k]], axis=0)
        out_refs[k][...] = both.astype(jnp.bfloat16)


def pack(tokens, out_grad, route_ids, route_weights, me_e, experts, cap):
    features = tokens.shape[1]
    message = jax.ShapeDtypeStruct((2 * PIECES * cap, features // PIECES), jnp.bfloat16)
    sources = (route_ids.T, route_weights.T, tokens, out_grad)
    return pl.pallas_call(
        functools.partial(pack_kernel, cap, experts),
        out_shape=[message] * experts,
        in_specs=[pl.BlockSpec(memory_space=pltpu.SMEM)] + [pl.BlockSpec(memory_space=pl.ANY)] * 4,
        out_specs=[pl.BlockSpec(memory_space=pltpu.VMEM)] * experts,
        scratch_shapes=[pltpu.VMEM(source.shape, source.dtype) for source in sources]
        + [pltpu.SemaphoreType.DMA((4,))],
        compiler_params=pltpu.CompilerParams(vmem_limit_bytes=60 * MIB),
    )(me_e.reshape(1), *sources)


def project_kernel(units, at_ref, gate_ref, up_ref, *refs):
    x_refs, out_ref = refs[:-1], refs[-1]
    at = at_ref[0] if gate_ref.shape[1] == units else pl.multiple_of(at_ref[0] * units, units)
    x = jnp.concatenate([ref[...] for ref in x_refs], axis=0)
    for i, ref in enumerate((gate_ref, up_ref)):
        weight = ref[...] if ref.shape[1] == units else ref[:, pl.ds(at, units)]
        out_ref[:, i * units : (i + 1) * units] = jnp.dot(
            x, weight, preferred_element_type=jnp.float32
        ).astype(out_ref.dtype)


def project(x_blocks, gate_weight, up_weight, part, n_parts, dtype):
    units = gate_weight.shape[1] // n_parts
    rows, depth = sum(x.shape[0] for x in x_blocks), x_blocks[0].shape[1]
    if units % 128:
        gate_weight = lax.dynamic_slice_in_dim(gate_weight, part * units, units, 1)
        up_weight = lax.dynamic_slice_in_dim(up_weight, part * units, units, 1)
    vmem = pl.BlockSpec(memory_space=pltpu.VMEM)
    return pl.pallas_call(
        functools.partial(project_kernel, units),
        out_shape=jax.ShapeDtypeStruct((rows, 2 * units), dtype),
        in_specs=[pl.BlockSpec(memory_space=pltpu.SMEM)] + [vmem] * (2 + len(x_blocks)),
        out_specs=vmem,
        compiler_params=pltpu.CompilerParams(vmem_limit_bytes=32 * MIB),
        cost_estimate=pl.CostEstimate(
            flops=4 * rows * depth * units,
            bytes_accessed=2 * rows * depth + 4 * depth * units,
            transcendentals=0,
        ),
    )(part.reshape(1), gate_weight, up_weight, *x_blocks)


def finish_kernel(n_got, n_blocks, keep_ref, *refs):
    got_refs, dy_refs = refs[:n_got], refs[n_got : n_got + n_blocks]
    out_ref, stage_ref, sems = refs[n_got + n_blocks :]
    total = keep_ref[...]
    for got in got_refs:
        total = total + got[...].astype(jnp.float32)
    units = total.shape[1] // 2
    gate, up = total[:, :units], total[:, units:]
    hidden = gate / (1.0 + jnp.exp(-gate)) * up
    hidden = hidden.T.astype(jnp.bfloat16)
    chunks, _, width = stage_ref.shape
    copies = []
    for c in range(chunks):
        columns = slice(c * width, (c + 1) * width)
        dy = jnp.concatenate([ref[:, columns] for ref in dy_refs], axis=0)
        stage_ref[c] = jnp.dot(hidden, dy, preferred_element_type=jnp.float32).astype(jnp.bfloat16)
        copies.append(pltpu.make_async_copy(stage_ref.at[c], out_ref.at[:, columns], sems.at[c]))
        copies[-1].start()
    for copy in copies:
        copy.wait()


def finish(keep, arrived, dy_blocks):
    units, features = keep.shape[1] // 2, dy_blocks[0].shape[1]
    vmem = pl.BlockSpec(memory_space=pltpu.VMEM)
    width = 512
    chunks = features // width
    return pl.pallas_call(
        functools.partial(finish_kernel, len(arrived), len(dy_blocks)),
        out_shape=jax.ShapeDtypeStruct((units, features), jnp.bfloat16),
        in_specs=[vmem] * (1 + len(arrived) + len(dy_blocks)),
        out_specs=pl.BlockSpec(memory_space=pl.ANY),
        scratch_shapes=[
            pltpu.VMEM((chunks, units, width), jnp.bfloat16),
            pltpu.SemaphoreType.DMA((chunks,)),
        ],
        compiler_params=pltpu.CompilerParams(vmem_limit_bytes=48 * MIB),
    )(keep, *arrived, *dy_blocks)


def per_device(tokens, out_grad, gate_weight, up_weight, route_ids, route_weights):
    n_dp, n_expert = lax.axis_size("dp"), lax.axis_size("expert")
    experts = n_expert // SPLIT
    depth = gate_weight.shape[0]
    cap = max(2, tokens.shape[0] * route_ids.shape[1] * 3 // (2 * N_ROUTED))
    me_d, me_s = lax.axis_index("dp"), lax.axis_index("expert")
    me_e = me_s // SPLIT

    def send(value, by_d, by_e, by_q):
        pairs = []
        for d in range(n_dp):
            for s in range(n_expert):
                e, q = s // SPLIT, s % SPLIT
                to = (e ^ by_e) * SPLIT + (q ^ by_q)
                pairs.append((d * n_expert + s, (d + by_d) % n_dp * n_expert + to))
        return lax.ppermute(value, AXES, pairs)

    messages = pack(tokens, out_grad, route_ids, route_weights, me_e, experts, cap)
    parts = [messages[0]] + [send(messages[k], 0, k, 0) for k in range(1, experts)]

    def unfold(part, first):
        return jnp.concatenate(
            [part[(first + j) * cap : (first + j + 1) * cap] for j in range(PIECES)], axis=1
        )

    held_x = jnp.concatenate([unfold(part, 0) for part in parts], axis=0)
    held_dy = jnp.concatenate([unfold(part, PIECES) for part in parts], axis=0)

    def x_for(by_d):
        return lax.dynamic_slice_in_dim(held_x, (me_d + by_d) % n_dp * depth, depth, 1)

    x_blocks, dy_blocks = {}, {}
    for by_d in reversed(range(n_dp)):
        x_part = x_for(by_d)
        x_blocks[by_d, 2] = send(x_part, by_d, 0, 2)
        x_blocks[by_d, 0] = send(x_part, by_d, 0, 0) if by_d else x_part
    for by_d in reversed(range(n_dp)):
        dy_blocks[by_d, 0] = send(held_dy, by_d, 0, 0) if by_d else held_dy
        dy_blocks[by_d, 2] = send(dy_blocks[by_d, 0], 0, 0, 2)

    def both_cores(blocks):
        other = {key: send(block, 0, 0, 1) for key, block in blocks.items()}
        keys = [(by_d, by_q) for by_d in range(n_dp) for by_q in (0, 2)]
        return [blocks[key] for key in keys], [other[key] for key in keys]

    x_own, x_other = both_cores(x_blocks)
    dy_own, dy_other = both_cores(dy_blocks)

    def x_rows(by_d):
        rows = []
        for blocks in (x_own, x_other):
            step = len(blocks) // n_dp
            rows += [blocks[(i - by_d * step) % len(blocks)] for i in range(len(blocks))]
        return rows

    arrived = []
    for by_d in range(1, n_dp):
        to = (me_d + by_d) % n_dp
        ready = project(x_rows(by_d), gate_weight, up_weight, to, n_dp, jnp.bfloat16)
        arrived.append(send(ready, by_d, 0, 0))
    keep = project(x_rows(0), gate_weight, up_weight, me_d, n_dp, jnp.float32)
    return finish(keep, arrived, dy_own + dy_other)


def solution(mesh):
    return jax.shard_map(
        per_device,
        mesh=mesh,
        in_specs=(
            P(("dp", "expert"), None),
            P(("dp", "expert"), None),
            P("dp", "expert"),
            P("dp", "expert"),
            P(("dp", "expert"), None),
            P(("dp", "expert"), None),
        ),
        out_specs=P(("expert", "dp"), None),
        check_vma=False,
    )
```

```python
import functools

import jax
import jax.numpy as jnp
from jax import lax
from jax.experimental import pallas as pl
from jax.experimental.pallas import tpu as pltpu
from jax.sharding import PartitionSpec as P

N_ROUTED = 256
SPLIT = 4
PIECES = 4
AXES = ("dp", "expert")
MIB = 1024 * 1024


def pack_kernel(cap, experts, me_ref, *refs):
    sources, out_refs = refs[:4], refs[4 : 4 + experts]
    held_refs, sems = refs[4 + experts : 8 + experts], refs[8 + experts]
    copies = [
        pltpu.make_async_copy(source, held, sems.at[i])
        for i, (source, held) in enumerate(zip(sources, held_refs))
    ]
    for copy in copies:
        copy.start()
    ids_ref, weights_ref, tokens_ref, grads_ref = held_refs
    rows, width = tokens_ref.shape[0], tokens_ref.shape[1] // PIECES
    copies[0].wait()
    copies[1].wait()
    ids, weights = ids_ref[...], weights_ref[...]
    chosen, scales = [], []
    for k in range(experts):
        match = ids == (me_ref[0] ^ k)
        chosen.append(jnp.max(jnp.where(match, 1.0, 0.0), axis=0, keepdims=True))
        scales.append(jnp.sum(jnp.where(match, weights, 0.0), axis=0, keepdims=True))
    flags = jnp.concatenate(chosen, axis=0)
    before = lax.broadcasted_iota(jnp.int32, (rows, rows), 0)
    after = lax.broadcasted_iota(jnp.int32, (rows, rows), 1)
    upper = jnp.where(before <= after, 1.0, 0.0).astype(jnp.bfloat16)
    rank = jnp.dot(flags.astype(jnp.bfloat16), upper, preferred_element_type=jnp.float32)
    height = PIECES * cap
    row = lax.broadcasted_iota(jnp.int32, (height, rows), 0)
    piece, slot = row // cap, row % cap
    picks, slot_scales = [], []
    for k in range(experts):
        place = jnp.where(chosen[k] > 0.0, rank[k : k + 1], 0.0).astype(jnp.int32)
        pick = place == slot + 1
        picks.append(jnp.where(pick, 1.0, 0.0))
        slot_scales.append(jnp.sum(jnp.where(pick, scales[k], 0.0), axis=1, keepdims=True))
    pick_all = jnp.concatenate(picks, axis=0)
    piece_all = jnp.concatenate([piece] * experts, axis=0)
    select = jnp.concatenate(
        [jnp.where(piece_all == j, pick_all, 0.0) for j in range(PIECES)], axis=1
    ).astype(jnp.bfloat16)

    def pieces(ref):
        return jnp.concatenate([ref[:, j * width : (j + 1) * width] for j in range(PIECES)], axis=0)

    copies[2].wait()
    rows_x = jnp.dot(select, pieces(tokens_ref), preferred_element_type=jnp.float32)
    copies[3].wait()
    rows_dy = jnp.dot(select, pieces(grads_ref), preferred_element_type=jnp.float32)
    for k in range(experts):
        at = slice(k * height, (k + 1) * height)
        both = jnp.concatenate([rows_x[at], rows_dy[at] * slot_scales[k]], axis=0)
        out_refs[k][...] = both.astype(jnp.bfloat16)


def pack(tokens, out_grad, route_ids, route_weights, me_e, experts, cap):
    features = tokens.shape[1]
    message = jax.ShapeDtypeStruct((2 * PIECES * cap, features // PIECES), jnp.bfloat16)
    sources = (route_ids.T, route_weights.T, tokens, out_grad)
    held = [pltpu.VMEM(source.shape, source.dtype) for source in sources]
    sources = [pltpu.with_memory_space_constraint(source, pltpu.HBM) for source in sources]
    return pl.pallas_call(
        functools.partial(pack_kernel, cap, experts),
        out_shape=[message] * experts,
        in_specs=[pl.BlockSpec(memory_space=pltpu.SMEM)] + [pl.BlockSpec(memory_space=pl.ANY)] * 4,
        out_specs=[pl.BlockSpec(memory_space=pltpu.VMEM)] * experts,
        scratch_shapes=held + [pltpu.SemaphoreType.DMA((4,))],
        compiler_params=pltpu.CompilerParams(vmem_limit_bytes=16 * MIB),
    )(me_e.reshape(1), *sources)


def project_kernel(n_weights, at_ref, *refs):
    weight_refs, x_refs, out_ref = refs[:n_weights], refs[n_weights:-1], refs[-1]
    x = jnp.concatenate([ref[...] for ref in x_refs], axis=0)
    width = out_ref.shape[1] // n_weights
    for i, ref in enumerate(weight_refs):
        if ref.shape[1] == width:
            weight = ref[...]
        else:
            weight = ref[:, pl.ds(pl.multiple_of(at_ref[0] * width, width), width)]
        out_ref[:, i * width : (i + 1) * width] = jnp.dot(
            x, weight, preferred_element_type=jnp.float32
        ).astype(out_ref.dtype)


def project(x_blocks, weights, part, units, dtype):
    rows, depth = sum(x.shape[0] for x in x_blocks), weights[0].shape[0]
    if units % 128 and len(weights) == 2:
        weights = [lax.dynamic_slice_in_dim(weight, part * units, units, 1) for weight in weights]
    vmem = pl.BlockSpec(memory_space=pltpu.VMEM)
    return pl.pallas_call(
        functools.partial(project_kernel, len(weights)),
        out_shape=jax.ShapeDtypeStruct((rows, 2 * units), dtype),
        in_specs=[pl.BlockSpec(memory_space=pltpu.SMEM)] + [vmem] * (len(weights) + len(x_blocks)),
        out_specs=vmem,
        compiler_params=pltpu.CompilerParams(vmem_limit_bytes=16 * MIB + 8 * rows * depth),
        cost_estimate=pl.CostEstimate(
            flops=4 * rows * depth * units,
            bytes_accessed=2 * rows * depth + 4 * depth * units,
            transcendentals=0,
        ),
    )(part.reshape(1), *weights, *x_blocks)


def finish_kernel(n_got, n_blocks, keep_ref, *refs):
    got_refs, dy_refs = refs[:n_got], refs[n_got : n_got + n_blocks]
    out_ref, stage_ref, sems = refs[n_got + n_blocks :]
    total = keep_ref[...]
    for got in got_refs:
        total = total + got[...].astype(jnp.float32)
    units = total.shape[1] // 2
    gate, up = total[:, :units], total[:, units:]
    hidden = gate / (1.0 + jnp.exp(-gate)) * up
    hidden = hidden.T.astype(jnp.bfloat16)
    chunks, _, width = stage_ref.shape
    copies = []
    for c in range(chunks):
        columns = slice(c * width, (c + 1) * width)
        dy = jnp.concatenate([ref[:, columns] for ref in dy_refs], axis=0)
        stage_ref[c] = jnp.dot(hidden, dy, preferred_element_type=jnp.float32).astype(jnp.bfloat16)
        copies.append(pltpu.make_async_copy(stage_ref.at[c], out_ref.at[:, columns], sems.at[c]))
        copies[-1].start()
    for copy in copies:
        copy.wait()


def finish(keep, arrived, dy_blocks):
    units, features = keep.shape[1] // 2, dy_blocks[0].shape[1]
    vmem = pl.BlockSpec(memory_space=pltpu.VMEM)
    width = 512
    chunks = features // width
    return pl.pallas_call(
        functools.partial(finish_kernel, len(arrived), len(dy_blocks)),
        out_shape=jax.ShapeDtypeStruct((units, features), jnp.bfloat16),
        in_specs=[vmem] * (1 + len(arrived) + len(dy_blocks)),
        out_specs=pl.BlockSpec(memory_space=pl.ANY),
        scratch_shapes=[
            pltpu.VMEM((chunks, units, width), jnp.bfloat16),
            pltpu.SemaphoreType.DMA((chunks,)),
        ],
        compiler_params=pltpu.CompilerParams(
            vmem_limit_bytes=8 * MIB + 4 * features * (keep.shape[0] + units)
        ),
    )(keep, *arrived, *dy_blocks)


def per_device(tokens, out_grad, gate_weight, up_weight, route_ids, route_weights):
    n_dp, n_expert = lax.axis_size("dp"), lax.axis_size("expert")
    experts = n_expert // SPLIT
    depth, units = gate_weight.shape[0], gate_weight.shape[1] // n_dp
    cap = max(2, tokens.shape[0] * route_ids.shape[1] * 3 // (2 * N_ROUTED))
    me_d, me_s = lax.axis_index("dp"), lax.axis_index("expert")
    me_e = me_s // SPLIT

    def send(value, by_d, by_e, by_q):
        pairs = []
        for d in range(n_dp):
            for s in range(n_expert):
                e, q = s // SPLIT, s % SPLIT
                to = (e ^ by_e) * SPLIT + (q ^ by_q)
                pairs.append((d * n_expert + s, (d + by_d) % n_dp * n_expert + to))
        return lax.ppermute(value, AXES, pairs)

    def after(value, *others):
        return lax.optimization_barrier((value, *others))[0]

    messages = pack(tokens, out_grad, route_ids, route_weights, me_e, experts, cap)
    parts = {0: messages[0]}
    for k in range(1, experts):
        parts[k] = send(messages[k], 0, k, 0)

    gate_from, up_from, _ = lax.optimization_barrier((gate_weight, up_weight, parts[1]))

    def columns_for(by_d):
        at = (me_d + by_d) % n_dp * units
        return jnp.concatenate(
            [lax.dynamic_slice_in_dim(weight, at, units, 1) for weight in (gate_from, up_from)], axis=1
        )

    def unfold(part, first):
        return jnp.concatenate(
            [part[(first + j) * cap : (first + j + 1) * cap] for j in range(PIECES)], axis=1
        )

    def held(ks, first):
        return jnp.concatenate([unfold(parts[k], first) for k in ks], axis=0)

    def half(rows, by_d):
        return lax.dynamic_slice_in_dim(rows, (me_d + by_d) % n_dp * depth, depth, 1)

    next_chips = [(by_d, 0) for by_d in range(1, n_dp)] + [(0, 2)]
    soon, late = range(experts // 2), range(experts // 2, experts)
    soon_x, soon_dy = held(soon, 0), held(soon, PIECES)
    early = {(by_d, by_q): send(soon_dy, by_d, 0, by_q) for by_d, by_q in next_chips}
    late_x = after(held(late, 0), *early.values())
    late_dy = after(held(late, PIECES), *early.values())
    held_x = jnp.concatenate([soon_x, late_x], axis=0)
    held_dy = jnp.concatenate([soon_dy, late_dy], axis=0)

    x_blocks, dy_blocks = {(0, 0): half(held_x, 0)}, {(0, 0): held_dy}
    for by_d in reversed(range(1, n_dp)):
        x_blocks[by_d, 2] = send(half(held_x, by_d), by_d, 0, 2)
    for by_d, by_q in next_chips:
        x_blocks[by_d, by_q] = send(half(held_x, by_d), by_d, 0, by_q)
    for by_d, by_q in next_chips:
        rows = send(late_dy, by_d, 0, by_q)
        dy_blocks[by_d, by_q] = jnp.concatenate([early[by_d, by_q], rows], axis=0)
    for by_d in range(1, n_dp):
        dy_blocks[by_d, 2] = send(dy_blocks[by_d, 0], 0, 0, 2)

    def both_cores(blocks):
        own = [blocks[by_d, by_q] for by_d in range(n_dp) for by_q in (0, 2)]
        return [own, [send(block, 0, 0, 1) for block in own]]

    x_lists, dy_lists = both_cores(x_blocks), both_cores(dy_blocks)

    def x_rows(by_d):
        rows = []
        for blocks in x_lists:
            step = len(blocks) // n_dp
            rows += [blocks[(i - by_d * step) % len(blocks)] for i in range(len(blocks))]
        return rows

    arrived = []
    for by_d in range(1, n_dp):
        ready = project(x_rows(by_d), [columns_for(by_d)], me_d, units, jnp.bfloat16)
        arrived.append(send(ready, by_d, 0, 0))
    keep = project(x_rows(0), [gate_weight, up_weight], me_d, units, jnp.float32)
    return finish(keep, arrived, [block for blocks in dy_lists for block in blocks])


def solution(mesh):
    return jax.shard_map(
        per_device,
        mesh=mesh,
        in_specs=(
            P(("dp", "expert"), None),
            P(("dp", "expert"), None),
            P("dp", "expert"),
            P("dp", "expert"),
            P(("dp", "expert"), None),
            P(("dp", "expert"), None),
        ),
        out_specs=P(("expert", "dp"), None),
        check_vma=False,
    )
```

```python
import functools

import jax
import jax.numpy as jnp
from jax import lax
from jax.experimental import pallas as pl
from jax.experimental.pallas import tpu as pltpu
from jax.sharding import PartitionSpec as P

N_ROUTED = 256
SPLIT = 4
PIECES = 4
AXES = ("dp", "expert")
MIB = 1024 * 1024


def pack_kernel(cap, experts, me_ref, *refs):
    sources, x_out_refs, dy_out_refs = refs[:4], refs[4 : 4 + experts], refs[4 + experts : -5]
    held_refs, sems = refs[-5:-1], refs[-1]
    copies = [
        pltpu.make_async_copy(source, held, sems.at[i])
        for i, (source, held) in enumerate(zip(sources, held_refs))
    ]
    for copy in copies:
        copy.start()
    ids_ref, weights_ref, tokens_ref, grads_ref = held_refs
    rows, width = tokens_ref.shape[0], tokens_ref.shape[1] // PIECES
    copies[0].wait()
    copies[1].wait()
    ids, weights = ids_ref[...], weights_ref[...]
    chosen, scales = [], []
    for k in range(experts):
        match = ids == (me_ref[0] ^ k)
        chosen.append(jnp.max(jnp.where(match, 1.0, 0.0), axis=0, keepdims=True))
        scales.append(jnp.sum(jnp.where(match, weights, 0.0), axis=0, keepdims=True))
    flags = jnp.concatenate(chosen, axis=0)
    before = lax.broadcasted_iota(jnp.int32, (rows, rows), 0)
    after = lax.broadcasted_iota(jnp.int32, (rows, rows), 1)
    upper = jnp.where(before <= after, 1.0, 0.0).astype(jnp.bfloat16)
    rank = jnp.dot(flags.astype(jnp.bfloat16), upper, preferred_element_type=jnp.float32)
    height = PIECES * cap
    row = lax.broadcasted_iota(jnp.int32, (height, rows), 0)
    piece, slot = row // cap, row % cap
    picks, slot_scales = [], []
    for k in range(experts):
        place = jnp.where(chosen[k] > 0.0, rank[k : k + 1], 0.0).astype(jnp.int32)
        pick = place == slot + 1
        picks.append(jnp.where(pick, 1.0, 0.0))
        slot_scales.append(jnp.sum(jnp.where(pick, scales[k], 0.0), axis=1, keepdims=True))
    pick_all = jnp.concatenate(picks, axis=0)
    piece_all = jnp.concatenate([piece] * experts, axis=0)
    select = jnp.concatenate(
        [jnp.where(piece_all == j, pick_all, 0.0) for j in range(PIECES)], axis=1
    ).astype(jnp.bfloat16)

    def pieces(ref):
        return jnp.concatenate([ref[:, j * width : (j + 1) * width] for j in range(PIECES)], axis=0)

    copies[2].wait()
    rows_x = jnp.dot(select, pieces(tokens_ref), preferred_element_type=jnp.float32)
    copies[3].wait()
    rows_dy = jnp.dot(select, pieces(grads_ref), preferred_element_type=jnp.float32)
    for k in range(experts):
        at = slice(k * height, (k + 1) * height)
        x_out_refs[k][...] = rows_x[at].astype(jnp.bfloat16)
        dy_out_refs[k][...] = (rows_dy[at] * slot_scales[k]).astype(jnp.bfloat16)


def pack(tokens, out_grad, route_ids, route_weights, me_e, experts, cap):
    features = tokens.shape[1]
    message = jax.ShapeDtypeStruct((PIECES * cap, features // PIECES), jnp.bfloat16)
    sources = (route_ids.T, route_weights.T, tokens, out_grad)
    held = [pltpu.VMEM(source.shape, source.dtype) for source in sources]
    sources = [pltpu.with_memory_space_constraint(source, pltpu.HBM) for source in sources]
    packed = pl.pallas_call(
        functools.partial(pack_kernel, cap, experts),
        out_shape=[message] * 2 * experts,
        in_specs=[pl.BlockSpec(memory_space=pltpu.SMEM)] + [pl.BlockSpec(memory_space=pl.ANY)] * 4,
        out_specs=[pl.BlockSpec(memory_space=pltpu.VMEM)] * 2 * experts,
        scratch_shapes=held + [pltpu.SemaphoreType.DMA((4,))],
        compiler_params=pltpu.CompilerParams(vmem_limit_bytes=16 * MIB),
    )(me_e.reshape(1), *sources)
    return packed[:experts], packed[experts:]


def project_kernel(n_weights, at_ref, *refs):
    weight_refs, x_refs, out_ref = refs[:n_weights], refs[n_weights:-1], refs[-1]
    x = jnp.concatenate([ref[...] for ref in x_refs], axis=0)
    width = out_ref.shape[1] // n_weights
    for i, ref in enumerate(weight_refs):
        if ref.shape[1] == width:
            weight = ref[...]
        else:
            weight = ref[:, pl.ds(pl.multiple_of(at_ref[0] * width, width), width)]
        out_ref[:, i * width : (i + 1) * width] = jnp.dot(
            x, weight, preferred_element_type=jnp.float32
        ).astype(out_ref.dtype)


def project(x_blocks, weights, part, units, dtype):
    rows, depth = sum(x.shape[0] for x in x_blocks), weights[0].shape[0]
    if units % 128 and len(weights) == 2:
        weights = [lax.dynamic_slice_in_dim(weight, part * units, units, 1) for weight in weights]
    vmem = pl.BlockSpec(memory_space=pltpu.VMEM)
    return pl.pallas_call(
        functools.partial(project_kernel, len(weights)),
        out_shape=jax.ShapeDtypeStruct((rows, 2 * units), dtype),
        in_specs=[pl.BlockSpec(memory_space=pltpu.SMEM)] + [vmem] * (len(weights) + len(x_blocks)),
        out_specs=vmem,
        compiler_params=pltpu.CompilerParams(vmem_limit_bytes=16 * MIB + 8 * rows * depth),
        cost_estimate=pl.CostEstimate(
            flops=4 * rows * depth * units,
            bytes_accessed=2 * rows * depth + 4 * depth * units,
            transcendentals=0,
        ),
    )(part.reshape(1), *weights, *x_blocks)


def finish_kernel(n_got, n_blocks, keep_ref, *refs):
    got_refs, dy_refs = refs[:n_got], refs[n_got : n_got + n_blocks]
    out_ref, stage_ref, sems = refs[n_got + n_blocks :]
    total = keep_ref[...]
    for got in got_refs:
        total = total + got[...].astype(jnp.float32)
    units = total.shape[1] // 2
    gate, up = total[:, :units], total[:, units:]
    hidden = gate / (1.0 + jnp.exp(-gate)) * up
    hidden = hidden.T.astype(jnp.bfloat16)
    chunks, _, width = stage_ref.shape
    copies = []
    for c in range(chunks):
        columns = slice(c * width, (c + 1) * width)
        dy = jnp.concatenate([ref[:, columns] for ref in dy_refs], axis=0)
        stage_ref[c] = jnp.dot(hidden, dy, preferred_element_type=jnp.float32).astype(jnp.bfloat16)
        copies.append(pltpu.make_async_copy(stage_ref.at[c], out_ref.at[:, columns], sems.at[c]))
        copies[-1].start()
    for copy in copies:
        copy.wait()


def finish(keep, arrived, dy_blocks):
    units, features = keep.shape[1] // 2, dy_blocks[0].shape[1]
    vmem = pl.BlockSpec(memory_space=pltpu.VMEM)
    width = 512
    chunks = features // width
    return pl.pallas_call(
        functools.partial(finish_kernel, len(arrived), len(dy_blocks)),
        out_shape=jax.ShapeDtypeStruct((units, features), jnp.bfloat16),
        in_specs=[vmem] * (1 + len(arrived) + len(dy_blocks)),
        out_specs=pl.BlockSpec(memory_space=pl.ANY),
        scratch_shapes=[
            pltpu.VMEM((chunks, units, width), jnp.bfloat16),
            pltpu.SemaphoreType.DMA((chunks,)),
        ],
        compiler_params=pltpu.CompilerParams(
            vmem_limit_bytes=8 * MIB + 4 * features * (keep.shape[0] + units)
        ),
    )(keep, *arrived, *dy_blocks)


def per_device(tokens, out_grad, gate_weight, up_weight, route_ids, route_weights):
    n_dp, n_expert = lax.axis_size("dp"), lax.axis_size("expert")
    experts = n_expert // SPLIT
    depth, units = gate_weight.shape[0], gate_weight.shape[1] // n_dp
    cap = max(2, tokens.shape[0] * route_ids.shape[1] * 3 // (2 * N_ROUTED))
    me_d, me_s = lax.axis_index("dp"), lax.axis_index("expert")
    me_e = me_s // SPLIT

    def send(value, by_d, by_e, by_q):
        pairs = []
        for d in range(n_dp):
            for s in range(n_expert):
                e, q = s // SPLIT, s % SPLIT
                to = (e ^ by_e) * SPLIT + (q ^ by_q)
                pairs.append((d * n_expert + s, (d + by_d) % n_dp * n_expert + to))
        return lax.ppermute(value, AXES, pairs)

    def after(value, *others):
        return lax.optimization_barrier((value, *others))[0]

    packed_x, packed_dy = pack(tokens, out_grad, route_ids, route_weights, me_e, experts, cap)

    def across_planes(packed):
        return [packed[0]] + [send(packed[k], 0, k, 0) for k in range(1, experts)]

    x_parts, dy_parts = across_planes(packed_x), across_planes(packed_dy)

    gate_from, up_from, _ = lax.optimization_barrier((gate_weight, up_weight, x_parts[1]))

    def columns_for(by_d):
        at = (me_d + by_d) % n_dp * units
        return jnp.concatenate(
            [lax.dynamic_slice_in_dim(weight, at, units, 1) for weight in (gate_from, up_from)], axis=1
        )

    def unfold(parts):
        return jnp.concatenate(
            [
                jnp.concatenate([part[j * cap : (j + 1) * cap] for j in range(PIECES)], axis=1)
                for part in parts
            ],
            axis=0,
        )

    held_x, held_dy = unfold(x_parts), unfold(dy_parts)

    def half(by_d):
        return lax.dynamic_slice_in_dim(held_x, (me_d + by_d) % n_dp * depth, depth, 1)

    next_chips = [(by_d, 0) for by_d in range(1, n_dp)] + [(0, 2)]
    x_blocks = {(0, 0): half(0)}
    for by_d in reversed(range(1, n_dp)):
        x_blocks[by_d, 2] = send(half(by_d), by_d, 0, 2)
    for by_d, by_q in next_chips:
        x_blocks[by_d, by_q] = send(half(by_d), by_d, 0, by_q)
    ready_dy = after(held_dy, x_blocks[1, 0])
    dy_blocks = {(0, 0): held_dy}
    for by_d, by_q in next_chips:
        dy_blocks[by_d, by_q] = send(ready_dy, by_d, 0, by_q)
    for by_d in range(1, n_dp):
        dy_blocks[by_d, 2] = send(dy_blocks[by_d, 0], 0, 0, 2)

    def both_cores(blocks):
        own = [blocks[by_d, by_q] for by_d in range(n_dp) for by_q in (0, 2)]
        return [own, [send(block, 0, 0, 1) for block in own]]

    x_lists, dy_lists = both_cores(x_blocks), both_cores(dy_blocks)

    def x_rows(by_d):
        rows = []
        for blocks in x_lists:
            step = len(blocks) // n_dp
            rows += [blocks[(i - by_d * step) % len(blocks)] for i in range(len(blocks))]
        return rows

    arrived = []
    for by_d in range(1, n_dp):
        ready = project(x_rows(by_d), [columns_for(by_d)], me_d, units, jnp.bfloat16)
        arrived.append(send(ready, by_d, 0, 0))
    keep = project(x_rows(0), [gate_weight, up_weight], me_d, units, jnp.float32)
    return finish(keep, arrived, [block for blocks in dy_lists for block in blocks])


def solution(mesh):
    return jax.shard_map(
        per_device,
        mesh=mesh,
        in_specs=(
            P(("dp", "expert"), None),
            P(("dp", "expert"), None),
            P("dp", "expert"),
            P("dp", "expert"),
            P(("dp", "expert"), None),
            P(("dp", "expert"), None),
        ),
        out_specs=P(("expert", "dp"), None),
        check_vma=False,
    )
```

```python
import functools

import jax
import jax.numpy as jnp
from jax import lax
from jax.experimental import pallas as pl
from jax.experimental.pallas import tpu as pltpu
from jax.sharding import PartitionSpec as P

N_ROUTED = 256
SPLIT = 4
PIECES = 4
AXES = ("dp", "expert")
MIB = 1024 * 1024


def pack_kernel(cap, experts, me_ref, *refs):
    sources, x_out_refs, dy_out_refs = refs[:4], refs[4 : 4 + experts], refs[4 + experts : -5]
    held_refs, sems = refs[-5:-1], refs[-1]
    copies = [
        pltpu.make_async_copy(source, held, sems.at[i])
        for i, (source, held) in enumerate(zip(sources, held_refs))
    ]
    for i in (0, 2, 1, 3):
        copies[i].start()
    ids_ref, weights_ref, tokens_ref, grads_ref = held_refs
    rows, width = tokens_ref.shape[0], tokens_ref.shape[1] // PIECES
    copies[0].wait()
    ids = ids_ref[...]
    matches, chosen = [], []
    for k in range(experts):
        matches.append(ids == (me_ref[0] ^ k))
        chosen.append(jnp.max(jnp.where(matches[k], 1.0, 0.0), axis=0, keepdims=True))
    flags = jnp.concatenate(chosen, axis=0)
    before = lax.broadcasted_iota(jnp.int32, (rows, rows), 0)
    after = lax.broadcasted_iota(jnp.int32, (rows, rows), 1)
    upper = jnp.where(before <= after, 1.0, 0.0).astype(jnp.bfloat16)
    rank = jnp.dot(flags.astype(jnp.bfloat16), upper, preferred_element_type=jnp.float32)
    height = PIECES * cap
    row = lax.broadcasted_iota(jnp.int32, (height, rows), 0)
    piece, slot = row // cap, row % cap
    picks = []
    for k in range(experts):
        place = jnp.where(chosen[k] > 0.0, rank[k : k + 1], 0.0).astype(jnp.int32)
        picks.append(jnp.where(place == slot + 1, 1.0, 0.0))
    pick_all = jnp.concatenate(picks, axis=0)
    piece_all = jnp.concatenate([piece] * experts, axis=0)
    select = jnp.concatenate(
        [jnp.where(piece_all == j, pick_all, 0.0) for j in range(PIECES)], axis=1
    ).astype(jnp.bfloat16)

    def pieces(ref):
        return jnp.concatenate([ref[:, j * width : (j + 1) * width] for j in range(PIECES)], axis=0)

    copies[2].wait()
    rows_x = jnp.dot(select, pieces(tokens_ref), preferred_element_type=jnp.float32)
    copies[1].wait()
    weights = weights_ref[...]
    slot_scales = []
    for k in range(experts):
        scale = jnp.sum(jnp.where(matches[k], weights, 0.0), axis=0, keepdims=True)
        slot_scales.append(jnp.sum(jnp.where(picks[k] > 0.0, scale, 0.0), axis=1, keepdims=True))
    copies[3].wait()
    rows_dy = jnp.dot(select, pieces(grads_ref), preferred_element_type=jnp.float32)
    for k in range(experts):
        at = slice(k * height, (k + 1) * height)
        x_out_refs[k][...] = rows_x[at].astype(jnp.bfloat16)
        dy_out_refs[k][...] = (rows_dy[at] * slot_scales[k]).astype(jnp.bfloat16)


def pack(tokens, out_grad, route_ids, route_weights, me_e, experts, cap):
    features = tokens.shape[1]
    message = jax.ShapeDtypeStruct((PIECES * cap, features // PIECES), jnp.bfloat16)
    sources = (route_ids.T, route_weights.T, tokens, out_grad)
    held = [pltpu.VMEM(source.shape, source.dtype) for source in sources]
    sources = [pltpu.with_memory_space_constraint(source, pltpu.HBM) for source in sources]
    packed = pl.pallas_call(
        functools.partial(pack_kernel, cap, experts),
        out_shape=[message] * 2 * experts,
        in_specs=[pl.BlockSpec(memory_space=pltpu.SMEM)] + [pl.BlockSpec(memory_space=pl.ANY)] * 4,
        out_specs=[pl.BlockSpec(memory_space=pltpu.VMEM)] * 2 * experts,
        scratch_shapes=held + [pltpu.SemaphoreType.DMA((4,))],
        compiler_params=pltpu.CompilerParams(vmem_limit_bytes=16 * MIB),
    )(me_e.reshape(1), *sources)
    return packed[:experts], packed[experts:]


def project_kernel(n_weights, at_ref, *refs):
    weight_refs, x_refs, out_ref = refs[:n_weights], refs[n_weights:-1], refs[-1]
    x = jnp.concatenate([ref[...] for ref in x_refs], axis=0)
    width = out_ref.shape[1] // n_weights
    for i, ref in enumerate(weight_refs):
        if ref.shape[1] == width:
            weight = ref[...]
        else:
            weight = ref[:, pl.ds(pl.multiple_of(at_ref[0] * width, width), width)]
        out_ref[:, i * width : (i + 1) * width] = jnp.dot(
            x, weight, preferred_element_type=jnp.float32
        ).astype(out_ref.dtype)


def project(x_blocks, weights, part, units, dtype):
    rows, depth = sum(x.shape[0] for x in x_blocks), weights[0].shape[0]
    if units % 128 and len(weights) == 2:
        weights = [lax.dynamic_slice_in_dim(weight, part * units, units, 1) for weight in weights]
    vmem = pl.BlockSpec(memory_space=pltpu.VMEM)
    return pl.pallas_call(
        functools.partial(project_kernel, len(weights)),
        out_shape=jax.ShapeDtypeStruct((rows, 2 * units), dtype),
        in_specs=[pl.BlockSpec(memory_space=pltpu.SMEM)] + [vmem] * (len(weights) + len(x_blocks)),
        out_specs=vmem,
        compiler_params=pltpu.CompilerParams(vmem_limit_bytes=16 * MIB + 8 * rows * depth),
        cost_estimate=pl.CostEstimate(
            flops=4 * rows * depth * units,
            bytes_accessed=2 * rows * depth + 4 * depth * units,
            transcendentals=0,
        ),
    )(part.reshape(1), *weights, *x_blocks)


def finish_kernel(n_got, n_blocks, keep_ref, *refs):
    got_refs, dy_refs = refs[:n_got], refs[n_got : n_got + n_blocks]
    out_ref, stage_ref, sems = refs[n_got + n_blocks :]
    total = keep_ref[...]
    for got in got_refs:
        total = total + got[...].astype(jnp.float32)
    units = total.shape[1] // 2
    gate, up = total[:, :units], total[:, units:]
    hidden = gate / (1.0 + jnp.exp(-gate)) * up
    hidden = hidden.T.astype(jnp.bfloat16)
    chunks, _, width = stage_ref.shape
    copies = []
    for c in range(chunks):
        columns = slice(c * width, (c + 1) * width)
        dy = jnp.concatenate([ref[:, columns] for ref in dy_refs], axis=0)
        stage_ref[c] = jnp.dot(hidden, dy, preferred_element_type=jnp.float32).astype(jnp.bfloat16)
        copies.append(pltpu.make_async_copy(stage_ref.at[c], out_ref.at[:, columns], sems.at[c]))
        copies[-1].start()
    for copy in copies:
        copy.wait()


def finish(keep, arrived, dy_blocks):
    units, features = keep.shape[1] // 2, dy_blocks[0].shape[1]
    vmem = pl.BlockSpec(memory_space=pltpu.VMEM)
    width = 512
    chunks = features // width
    return pl.pallas_call(
        functools.partial(finish_kernel, len(arrived), len(dy_blocks)),
        out_shape=jax.ShapeDtypeStruct((units, features), jnp.bfloat16),
        in_specs=[vmem] * (1 + len(arrived) + len(dy_blocks)),
        out_specs=pl.BlockSpec(memory_space=pl.ANY),
        scratch_shapes=[
            pltpu.VMEM((chunks, units, width), jnp.bfloat16),
            pltpu.SemaphoreType.DMA((chunks,)),
        ],
        compiler_params=pltpu.CompilerParams(
            vmem_limit_bytes=8 * MIB + 4 * features * (keep.shape[0] + units)
        ),
    )(keep, *arrived, *dy_blocks)


def per_device(tokens, out_grad, gate_weight, up_weight, route_ids, route_weights):
    n_dp, n_expert = lax.axis_size("dp"), lax.axis_size("expert")
    experts = n_expert // SPLIT
    depth, units = gate_weight.shape[0], gate_weight.shape[1] // n_dp
    cap = max(2, tokens.shape[0] * route_ids.shape[1] * 3 // (2 * N_ROUTED))
    me_d, me_s = lax.axis_index("dp"), lax.axis_index("expert")
    me_e = me_s // SPLIT

    def send(value, by_d, by_e, by_q):
        pairs = []
        for d in range(n_dp):
            for s in range(n_expert):
                e, q = s // SPLIT, s % SPLIT
                to = (e ^ by_e) * SPLIT + (q ^ by_q)
                pairs.append((d * n_expert + s, (d + by_d) % n_dp * n_expert + to))
        return lax.ppermute(value, AXES, pairs)

    def after(value, *others):
        return lax.optimization_barrier((value, *others))[0]

    packed_x, packed_dy = pack(tokens, out_grad, route_ids, route_weights, me_e, experts, cap)

    def across_planes(packed):
        return [packed[0]] + [send(packed[k], 0, k, 0) for k in range(1, experts)]

    x_parts, dy_parts = across_planes(packed_x), across_planes(packed_dy)

    gate_from, up_from, _ = lax.optimization_barrier((gate_weight, up_weight, x_parts[1]))

    def columns_for(by_d):
        at = (me_d + by_d) % n_dp * units
        return jnp.concatenate(
            [lax.dynamic_slice_in_dim(weight, at, units, 1) for weight in (gate_from, up_from)], axis=1
        )

    def unfold(parts):
        return jnp.concatenate(
            [
                jnp.concatenate([part[j * cap : (j + 1) * cap] for j in range(PIECES)], axis=1)
                for part in parts
            ],
            axis=0,
        )

    held_x, held_dy = unfold(x_parts), unfold(dy_parts)

    def half(by_d):
        return lax.dynamic_slice_in_dim(held_x, (me_d + by_d) % n_dp * depth, depth, 1)

    next_chips = [(by_d, 0) for by_d in range(1, n_dp)] + [(0, 2)]
    x_blocks = {(0, 0): half(0)}
    for by_d in reversed(range(1, n_dp)):
        x_blocks[by_d, 2] = send(half(by_d), by_d, 0, 2)
    for by_d, by_q in next_chips:
        x_blocks[by_d, by_q] = send(half(by_d), by_d, 0, by_q)
    ready_dy = after(held_dy, x_blocks[1, 0])
    dy_blocks = {(0, 0): held_dy}
    for by_d, by_q in next_chips:
        dy_blocks[by_d, by_q] = send(ready_dy, by_d, 0, by_q)
    for by_d in range(1, n_dp):
        dy_blocks[by_d, 2] = send(dy_blocks[by_d, 0], 0, 0, 2)

    def both_cores(blocks):
        own = [blocks[by_d, by_q] for by_d in range(n_dp) for by_q in (0, 2)]
        return [own, [send(block, 0, 0, 1) for block in own]]

    x_lists, dy_lists = both_cores(x_blocks), both_cores(dy_blocks)

    def x_rows(by_d):
        rows = []
        for blocks in x_lists:
            step = len(blocks) // n_dp
            rows += [blocks[(i - by_d * step) % len(blocks)] for i in range(len(blocks))]
        return rows

    arrived = []
    for by_d in range(1, n_dp):
        ready = project(x_rows(by_d), [columns_for(by_d)], me_d, units, jnp.bfloat16)
        arrived.append(send(ready, by_d, 0, 0))
    keep = project(x_rows(0), [gate_weight, up_weight], me_d, units, jnp.float32)
    return finish(keep, arrived, [block for blocks in dy_lists for block in blocks])


def solution(mesh):
    return jax.shard_map(
        per_device,
        mesh=mesh,
        in_specs=(
            P(("dp", "expert"), None),
            P(("dp", "expert"), None),
            P("dp", "expert"),
            P("dp", "expert"),
            P(("dp", "expert"), None),
            P(("dp", "expert"), None),
        ),
        out_specs=P(("expert", "dp"), None),
        check_vma=False,
    )
```

```python
import functools

import jax
import jax.numpy as jnp
from jax import lax
from jax.experimental import pallas as pl
from jax.experimental.pallas import tpu as pltpu
from jax.sharding import PartitionSpec as P

N_ROUTED = 256
SPLIT = 4
PIECES = 4
AXES = ("dp", "expert")
MIB = 1024 * 1024


def pack_kernel(cap, experts, me_ref, *refs):
    sources, x_out_refs, dy_out_refs = refs[:4], refs[4 : 4 + experts], refs[4 + experts : -5]
    held_refs, sems = refs[-5:-1], refs[-1]
    copies = [
        pltpu.make_async_copy(source, held, sems.at[i])
        for i, (source, held) in enumerate(zip(sources, held_refs))
    ]
    for copy in copies:
        copy.start()
    ids_ref, weights_ref, tokens_ref, grads_ref = held_refs
    rows, width = tokens_ref.shape[0], tokens_ref.shape[1] // PIECES
    copies[0].wait()
    copies[1].wait()
    ids, weights = ids_ref[...], weights_ref[...]
    chosen, scales = [], []
    for k in range(experts):
        match = ids == (me_ref[0] ^ k)
        chosen.append(jnp.max(jnp.where(match, 1.0, 0.0), axis=0, keepdims=True))
        scales.append(jnp.sum(jnp.where(match, weights, 0.0), axis=0, keepdims=True))
    flags = jnp.concatenate(chosen, axis=0)
    before = lax.broadcasted_iota(jnp.int32, (rows, rows), 0)
    after = lax.broadcasted_iota(jnp.int32, (rows, rows), 1)
    upper = jnp.where(before <= after, 1.0, 0.0).astype(jnp.bfloat16)
    rank = jnp.dot(flags.astype(jnp.bfloat16), upper, preferred_element_type=jnp.float32)
    height = PIECES * cap
    row = lax.broadcasted_iota(jnp.int32, (height, rows), 0)
    piece, slot = row // cap, row % cap
    picks, slot_scales = [], []
    for k in range(experts):
        place = jnp.where(chosen[k] > 0.0, rank[k : k + 1], 0.0).astype(jnp.int32)
        pick = place == slot + 1
        picks.append(jnp.where(pick, 1.0, 0.0))
        slot_scales.append(jnp.sum(jnp.where(pick, scales[k], 0.0), axis=1, keepdims=True))
    pick_all = jnp.concatenate(picks, axis=0)
    piece_all = jnp.concatenate([piece] * experts, axis=0)
    select = jnp.concatenate(
        [jnp.where(piece_all == j, pick_all, 0.0) for j in range(PIECES)], axis=1
    ).astype(jnp.bfloat16)

    def pieces(ref):
        return jnp.concatenate([ref[:, j * width : (j + 1) * width] for j in range(PIECES)], axis=0)

    copies[2].wait()
    rows_x = jnp.dot(select, pieces(tokens_ref), preferred_element_type=jnp.float32)
    copies[3].wait()
    rows_dy = jnp.dot(select, pieces(grads_ref), preferred_element_type=jnp.float32)
    for k in range(experts):
        at = slice(k * height, (k + 1) * height)
        x_out_refs[k][...] = rows_x[at].astype(jnp.bfloat16)
        dy_out_refs[k][...] = (rows_dy[at] * slot_scales[k]).astype(jnp.bfloat16)


def pack(tokens, out_grad, route_ids, route_weights, me_e, experts, cap):
    features = tokens.shape[1]
    message = jax.ShapeDtypeStruct((PIECES * cap, features // PIECES), jnp.bfloat16)
    sources = (route_ids.T, route_weights.T, tokens, out_grad)
    held = [pltpu.VMEM(source.shape, source.dtype) for source in sources]
    sources = [pltpu.with_memory_space_constraint(source, pltpu.HBM) for source in sources]
    packed = pl.pallas_call(
        functools.partial(pack_kernel, cap, experts),
        out_shape=[message] * 2 * experts,
        in_specs=[pl.BlockSpec(memory_space=pltpu.SMEM)] + [pl.BlockSpec(memory_space=pl.ANY)] * 4,
        out_specs=[pl.BlockSpec(memory_space=pltpu.VMEM)] * 2 * experts,
        scratch_shapes=held + [pltpu.SemaphoreType.DMA((4,))],
        compiler_params=pltpu.CompilerParams(vmem_limit_bytes=16 * MIB),
    )(me_e.reshape(1), *sources)
    return packed[:experts], packed[experts:]


def project_kernel(n_weights, at_ref, *refs):
    weight_refs, x_refs, out_ref = refs[:n_weights], refs[n_weights:-1], refs[-1]
    x = jnp.concatenate([ref[...] for ref in x_refs], axis=0)
    width = out_ref.shape[1] // n_weights
    for i, ref in enumerate(weight_refs):
        if ref.shape[1] == width:
            weight = ref[...]
        else:
            weight = ref[:, pl.ds(pl.multiple_of(at_ref[0] * width, width), width)]
        out_ref[:, i * width : (i + 1) * width] = jnp.dot(
            x, weight, preferred_element_type=jnp.float32
        ).astype(out_ref.dtype)


def project(x_blocks, weights, part, units, dtype):
    rows, depth = sum(x.shape[0] for x in x_blocks), weights[0].shape[0]
    if units % 128 and len(weights) == 2:
        weights = [lax.dynamic_slice_in_dim(weight, part * units, units, 1) for weight in weights]
    vmem = pl.BlockSpec(memory_space=pltpu.VMEM)
    return pl.pallas_call(
        functools.partial(project_kernel, len(weights)),
        out_shape=jax.ShapeDtypeStruct((rows, 2 * units), dtype),
        in_specs=[pl.BlockSpec(memory_space=pltpu.SMEM)] + [vmem] * (len(weights) + len(x_blocks)),
        out_specs=vmem,
        compiler_params=pltpu.CompilerParams(vmem_limit_bytes=16 * MIB + 8 * rows * depth),
        cost_estimate=pl.CostEstimate(
            flops=4 * rows * depth * units,
            bytes_accessed=2 * rows * depth + 4 * depth * units,
            transcendentals=0,
        ),
    )(part.reshape(1), *weights, *x_blocks)


def finish_kernel(n_got, n_blocks, keep_ref, *refs):
    got_refs, dy_refs = refs[:n_got], refs[n_got : n_got + n_blocks]
    out_ref, stage_ref, sems = refs[n_got + n_blocks :]
    total = keep_ref[...]
    for got in got_refs:
        total = total + got[...].astype(jnp.float32)
    units = total.shape[1] // 2
    gate, up = total[:, :units], total[:, units:]
    hidden = gate / (1.0 + jnp.exp(-gate)) * up
    hidden = hidden.T.astype(jnp.bfloat16)
    chunks, _, width = stage_ref.shape
    copies = []
    for c in range(chunks):
        columns = slice(c * width, (c + 1) * width)
        dy = jnp.concatenate([ref[:, columns] for ref in dy_refs], axis=0)
        stage_ref[c] = jnp.dot(hidden, dy, preferred_element_type=jnp.float32).astype(jnp.bfloat16)
        copies.append(pltpu.make_async_copy(stage_ref.at[c], out_ref.at[:, columns], sems.at[c]))
        copies[-1].start()
    for copy in copies:
        copy.wait()


def finish(keep, arrived, dy_blocks):
    units, features = keep.shape[1] // 2, dy_blocks[0].shape[1]
    vmem = pl.BlockSpec(memory_space=pltpu.VMEM)
    width = 512
    chunks = features // width
    return pl.pallas_call(
        functools.partial(finish_kernel, len(arrived), len(dy_blocks)),
        out_shape=jax.ShapeDtypeStruct((units, features), jnp.bfloat16),
        in_specs=[vmem] * (1 + len(arrived) + len(dy_blocks)),
        out_specs=pl.BlockSpec(memory_space=pl.ANY),
        scratch_shapes=[
            pltpu.VMEM((chunks, units, width), jnp.bfloat16),
            pltpu.SemaphoreType.DMA((chunks,)),
        ],
        compiler_params=pltpu.CompilerParams(
            vmem_limit_bytes=8 * MIB + 4 * features * (keep.shape[0] + units)
        ),
    )(keep, *arrived, *dy_blocks)


def per_device(tokens, out_grad, gate_weight, up_weight, route_ids, route_weights):
    n_dp, n_expert = lax.axis_size("dp"), lax.axis_size("expert")
    experts = n_expert // SPLIT
    depth, units = gate_weight.shape[0], gate_weight.shape[1] // n_dp
    cap = max(2, tokens.shape[0] * route_ids.shape[1] * 3 // (2 * N_ROUTED))
    me_d, me_s = lax.axis_index("dp"), lax.axis_index("expert")
    me_e = me_s // SPLIT

    def send(value, by_d, by_e, by_q):
        pairs = []
        for d in range(n_dp):
            for s in range(n_expert):
                e, q = s // SPLIT, s % SPLIT
                to = (e ^ by_e) * SPLIT + (q ^ by_q)
                pairs.append((d * n_expert + s, (d + by_d) % n_dp * n_expert + to))
        return lax.ppermute(value, AXES, pairs)

    def after(value, *others):
        return lax.optimization_barrier((value, *others))[0]

    packed_x, packed_dy = pack(tokens, out_grad, route_ids, route_weights, me_e, experts, cap)

    def across_planes(packed):
        return [packed[0]] + [send(packed[k], 0, k, 0) for k in range(1, experts)]

    x_parts, dy_parts = across_planes(packed_x), across_planes(packed_dy)

    gate_from, up_from, _ = lax.optimization_barrier((gate_weight, up_weight, x_parts[1]))

    def columns_for(by_d):
        at = (me_d + by_d) % n_dp * units
        return jnp.concatenate(
            [lax.dynamic_slice_in_dim(weight, at, units, 1) for weight in (gate_from, up_from)], axis=1
        )

    def unfold(parts):
        return jnp.concatenate(
            [
                jnp.concatenate([part[j * cap : (j + 1) * cap] for j in range(PIECES)], axis=1)
                for part in parts
            ],
            axis=0,
        )

    held_x, held_dy = unfold(x_parts), unfold(dy_parts)

    def half(by_d):
        return lax.dynamic_slice_in_dim(held_x, (me_d + by_d) % n_dp * depth, depth, 1)

    next_chips = [(by_d, 0) for by_d in range(1, n_dp)] + [(0, 2)]
    x_blocks = {(0, 0): half(0)}
    for by_d in reversed(range(1, n_dp)):
        x_blocks[by_d, 2] = send(half(by_d), by_d, 0, 2)
    for by_d, by_q in next_chips:
        x_blocks[by_d, by_q] = send(half(by_d), by_d, 0, by_q)
    ready_dy = after(held_dy, x_blocks[1, 0])
    dy_blocks = {(0, 0): held_dy}
    for by_d, by_q in next_chips:
        dy_blocks[by_d, by_q] = send(ready_dy, by_d, 0, by_q)
    for by_d in range(1, n_dp):
        dy_blocks[by_d, 2] = send(dy_blocks[by_d, 0], 0, 0, 2)

    def both_cores(blocks):
        own = [blocks[by_d, by_q] for by_d in range(n_dp) for by_q in (0, 2)]
        return [own, [send(block, 0, 0, 1) for block in own]]

    for by_d in range(1, n_dp):
        for by_q in (0, 2):
            x_blocks[by_d, by_q] = after(x_blocks[by_d, by_q], x_blocks[0, 2])
    x_lists, dy_lists = both_cores(x_blocks), both_cores(dy_blocks)

    def x_rows(by_d):
        rows = []
        for blocks in x_lists:
            step = len(blocks) // n_dp
            rows += [blocks[(i - by_d * step) % len(blocks)] for i in range(len(blocks))]
        return rows

    arrived = []
    for by_d in range(1, n_dp):
        ready = project(x_rows(by_d), [columns_for(by_d)], me_d, units, jnp.bfloat16)
        arrived.append(send(ready, by_d, 0, 0))
    keep = project(x_rows(0), [gate_weight, up_weight], me_d, units, jnp.float32)
    return finish(keep, arrived, [block for blocks in dy_lists for block in blocks])


def solution(mesh):
    return jax.shard_map(
        per_device,
        mesh=mesh,
        in_specs=(
            P(("dp", "expert"), None),
            P(("dp", "expert"), None),
            P("dp", "expert"),
            P("dp", "expert"),
            P(("dp", "expert"), None),
            P(("dp", "expert"), None),
        ),
        out_specs=P(("expert", "dp"), None),
        check_vma=False,
    )
```
